32 devices in a mesh: dp: 2 (over y), ctx: 8 (over z, core), head: 2 (over x).
Axes of the slice: x: 2, y: 2, z: 4, core: 2. Of those that a mesh axis runs over, the one named last changes fastest.
Arguments:
- queries: bfloat16 [2, 2048, 2048], P('dp', 'ctx', 'head'), may hold values from -35 to 35
- key_rows: bfloat16 [2, 2048, 2048], P('dp', 'ctx', 'head'), may hold values from -6 to 6
- value_rows: bfloat16 [2, 2048, 2048], P('dp', 'ctx', 'head'), may hold values from -6 to 6
- sink_logits: float32 [16], P('head'), may hold values from 4 to 9
- partner: int32 [3, 8], replicated, may hold values from 0 to 7, as said below
- block_pick: int32 [2, 3, 8], P('dp'), may hold values from 0 to 1
- out_grad: bfloat16 [2, 2048, 2048], P('dp', 'ctx', 'head'), may hold values from -18 to 18
Outputs:
- attention: bfloat16 [2, 2048, 2048], P('dp', 'ctx', 'head')
- query_grad: bfloat16 [2, 2048, 2048], P('dp', 'ctx', 'head')
- key_grad: bfloat16 [2, 2048, 2048], P('dp', 'ctx', 'head')
- value_grad: bfloat16 [2, 2048, 2048], P('dp', 'ctx', 'head')
- sink_grad: float32 [16], P('head')
The draws below stay inside these ranges and needn't reach their ends.
Inputs may be any that keep to these rules, and one draw needn't show every extreme that they name: partner[r, i] = i XOR partner[r, 0] for every round r, and partner[r, 0] is a power of two: each round pairs the indices of ctx that differ in one bit.
All inputs are finite; a program needn't handle non-finite values.
Results may differ from the reference program's by a relative error of at most 0.0093.
Values may be sent and summed in bfloat16 or wider, within the bound.
A program may use at most 128 MiB of HBM per device.

```python
import math
import jax
import jax.numpy as jnp
from jax import lax

HEADS = 16
HD = 128
BLOCK = 128
ROUNDS = 3
TOK_DEV = 256
LENGTH = 2048
DOCS = 2
CTX_BITS = 3
N_CTX = 8


def joint_rows(key):
    full_shape = (DOCS, LENGTH, HEADS * HD)
    first_key = jax.random.fold_in(key, 101)
    second_key = jax.random.fold_in(key, 202)
    query_full = jnp.clip(jax.random.normal(first_key, full_shape, jnp.float32), -6.0, 6.0)
    key_full = jnp.clip(jax.random.normal(second_key, full_shape, jnp.float32), -6.0, 6.0)
    return (query_full, key_full)


def draw_queries(key, part):
    return joint_rows(key)[0].astype(jnp.bfloat16)


def draw_key_rows(key, part):
    return joint_rows(key)[1].astype(jnp.bfloat16)


def draw_out_grad(key, part):
    full_shape = (DOCS, LENGTH, HEADS * HD)
    position = jnp.arange(LENGTH, dtype=jnp.float32)[None, :, None] / max(LENGTH - 1, 1)
    document = jnp.arange(DOCS, dtype=jnp.float32)[:, None, None] / max(DOCS - 1, 1)
    base_draw = jnp.clip(jax.random.normal(key, full_shape, jnp.float32), -6.0, 6.0)
    rising = (1.0 + 2.0 * position) * (1.0 + 2.0 * document) / 3.0
    return (base_draw * rising).astype(jnp.bfloat16)


def draw_partner(key, part):
    bit_places = jax.random.randint(key, (ROUNDS, 1), 0, CTX_BITS, dtype=jnp.int32)
    xor_masks = jnp.left_shift(jnp.ones((ROUNDS, 1), jnp.int32), bit_places)
    return jnp.bitwise_xor(jnp.arange(N_CTX, dtype=jnp.int32)[None, :], xor_masks).astype(jnp.int32)


def plant(values, rng, low, high):
    longest = values.shape.index(max(values.shape))
    spots = []
    for shift in (0, 1):
        where = [jax.random.randint(jax.random.fold_in(rng, axis), (), 0, length) for axis, length in enumerate(values.shape)]
        where[longest] = (where[longest] + shift) % values.shape[longest]
        spots.append(tuple(where))
    return values.at[spots[0]].set(low).at[spots[1]].set(high)


def levels(own_key, extent, split, low, largest):
    def one(dim, parts):
        steps = jax.random.uniform(jax.random.fold_in(jax.random.fold_in(own_key, 6), dim), (parts,), jnp.float32, low / len(split), largest / len(split))
        return jnp.repeat(jnp.exp(steps), extent[dim] // parts).reshape((-1,) + (1,) * (len(extent) - dim - 1))

    gain = one(*split[0])
    for cut in split[1:]:
        gain = gain * one(*cut)
    return gain


def normal_values(stream_key, shape, scale, most, split=(), kind=jnp.bfloat16):
    values = scale * jax.random.normal(stream_key, shape, jnp.float32)
    if split:
        values = values * levels(stream_key, shape, split, -0.22, 0.18)
    return jnp.clip(values, -most, most).astype(kind)


def setup_inputs(seed: int = 0) -> dict:
    keys = jax.random.split(jax.random.key(seed), 8)
    queries = draw_queries(jax.random.fold_in(keys[7], 71), 0)
    key_rows = draw_key_rows(jax.random.fold_in(keys[7], 71), 0)
    value_rows = normal_values(keys[2], (DOCS, LENGTH, HEADS * HD), 1.0, 6.0, ((0, 2), (1, 8), (2, 2)))
    sink_logits = jnp.clip(4.0 + 5.0 * jax.random.uniform(keys[3], (HEADS,), jnp.float32) ** levels(keys[3], (HEADS,), ((0, 2),), -0.2, 0.2), 4.0, 9.0)
    partner = draw_partner(jax.random.fold_in(keys[7], 71), 0)
    block_pick = plant(jax.random.randint(keys[5], (DOCS, ROUNDS, N_CTX), 0, TOK_DEV // BLOCK), jax.random.fold_in(keys[5], 1), 0, (TOK_DEV // BLOCK) - 1).astype(jnp.int32)
    out_grad = draw_out_grad(jax.random.fold_in(keys[7], 71), 0)
    return dict(queries=queries, key_rows=key_rows, value_rows=value_rows, sink_logits=sink_logits, partner=partner, block_pick=block_pick, out_grad=out_grad)


def as_rounded(values):
    return lax.optimization_barrier(values.astype(jnp.bfloat16)).astype(jnp.float32)

def head_pass(query_one, key_one, value_one, grad_one, sink_one, pick_doc, partner):
    total_blocks = LENGTH // BLOCK
    shard_blocks = TOK_DEV // BLOCK
    scaling = HD ** (-0.5)
    query_blocks = query_one.reshape(total_blocks, BLOCK, HD).astype(jnp.float32)
    key_blocks = key_one.reshape(total_blocks, BLOCK, HD)
    value_blocks = value_one.reshape(total_blocks, BLOCK, HD)
    block_ids = jnp.arange(total_blocks, dtype=jnp.int32)
    owner = block_ids // shard_blocks
    random_cols = [(partner[number][owner] * shard_blocks + pick_doc[number][owner]).astype(jnp.int32) for number in range(ROUNDS)]
    slot_ids = jnp.stack([jnp.zeros_like(block_ids), jnp.full_like(block_ids, total_blocks - 1), jnp.clip(block_ids - 1, 0, total_blocks - 1), block_ids, jnp.clip(block_ids + 1, 0, total_blocks - 1)] + random_cols, axis=1).astype(jnp.int32)
    always = block_ids >= 0
    slot_valid = jnp.stack([always, always, block_ids != 1, always, block_ids != total_blocks - 2] + [always] * ROUNDS, axis=1)
    slot_keys = key_blocks[slot_ids].astype(jnp.float32)
    slot_values = value_blocks[slot_ids].astype(jnp.float32)
    scores = scaling * jnp.einsum('nqd,nskd->nqsk', query_blocks, slot_keys)
    scores = jnp.where(slot_valid[:, None, :, None], scores, -jnp.inf)
    row_top = jnp.maximum(sink_one, lax.optimization_barrier(jnp.max(scores, axis=(2, 3))))
    expo = jnp.exp(scores - row_top[:, :, None, None])
    row_total = jnp.exp(sink_one - row_top) + lax.optimization_barrier(jnp.sum(expo, axis=(2, 3)))
    weights = as_rounded(expo)
    regular_out = jnp.einsum('nqsk,nskd->nqd', weights, slot_values) / row_total[:, :, None]
    global_query = jnp.concatenate([query_one[:BLOCK], query_one[LENGTH - BLOCK:]], axis=0)
    global_scores = scaling * jnp.dot(global_query, key_one.T, preferred_element_type=jnp.float32)
    global_top = jnp.maximum(sink_one, lax.optimization_barrier(jnp.max(global_scores, axis=1)))
    global_expo = jnp.exp(global_scores - global_top[:, None])
    global_total = jnp.exp(sink_one - global_top) + lax.optimization_barrier(jnp.sum(global_expo, axis=1))
    global_out = jnp.dot(global_expo.astype(jnp.bfloat16), value_one, preferred_element_type=jnp.float32) / global_total[:, None]
    full_out = regular_out.reshape(LENGTH, HD)
    full_out = full_out.at[:BLOCK].set(global_out[:BLOCK]).at[LENGTH - BLOCK:].set(global_out[BLOCK:])
    attention = full_out.astype(jnp.bfloat16)
    grad_full = grad_one.astype(jnp.float32)
    row_delta = lax.optimization_barrier(jnp.sum(grad_full * attention.astype(jnp.float32), axis=1))
    row_blocks = jnp.arange(LENGTH) // BLOCK
    regular_rows = (row_blocks != 0) & (row_blocks != total_blocks - 1)
    grad_regular = jnp.where(regular_rows[:, None], grad_full, 0.0).reshape(total_blocks, BLOCK, HD)
    delta_regular = jnp.where(regular_rows, row_delta, 0.0).reshape(total_blocks, BLOCK)
    row_lse = row_top + jnp.log(row_total)
    probs = jnp.exp(scores - row_lse[:, :, None, None])
    prob_half = as_rounded(probs)
    prob_grad = jnp.einsum('nqd,nskd->nqsk', grad_regular, slot_values)
    score_grad = as_rounded(probs * (prob_grad - delta_regular[:, :, None, None]))
    query_regular = scaling * jnp.einsum('nqsk,nskd->nqd', score_grad, slot_keys)
    key_slots = scaling * jnp.einsum('nqsk,nqd->nskd', score_grad, query_blocks)
    value_slots = jnp.einsum('nqsk,nqd->nskd', prob_half, grad_regular)
    key_acc = jnp.zeros((total_blocks, BLOCK, HD), jnp.float32).at[slot_ids[:, :5]].add(key_slots[:, :5])
    value_acc = jnp.zeros((total_blocks, BLOCK, HD), jnp.float32).at[slot_ids[:, :5]].add(value_slots[:, :5])
    targets = slot_ids[:, 5:].reshape(N_CTX, shard_blocks, ROUNDS)[:, 0]
    key_random = as_rounded(key_slots[:, 5:].reshape(N_CTX, shard_blocks, ROUNDS, BLOCK, HD).sum(axis=1))
    value_random = as_rounded(value_slots[:, 5:].reshape(N_CTX, shard_blocks, ROUNDS, BLOCK, HD).sum(axis=1))
    key_acc = key_acc.at[targets].add(key_random)
    value_acc = value_acc.at[targets].add(value_random)
    global_lse = global_top + jnp.log(global_total)
    global_probs = jnp.exp(global_scores - global_lse[:, None])
    global_grad = jnp.concatenate([grad_one[:BLOCK], grad_one[LENGTH - BLOCK:]], axis=0)
    global_att = jnp.concatenate([attention[:BLOCK], attention[LENGTH - BLOCK:]], axis=0)
    global_delta = lax.optimization_barrier(jnp.sum(global_grad.astype(jnp.float32) * global_att.astype(jnp.float32), axis=1))
    global_dp = jnp.dot(global_grad, value_one.T, preferred_element_type=jnp.float32)
    global_ds = (global_probs * (global_dp - global_delta[:, None])).astype(jnp.bfloat16)
    global_dq = scaling * jnp.dot(global_ds, key_one, preferred_element_type=jnp.float32)
    key_total = key_acc.reshape(LENGTH, HD) + scaling * jnp.dot(global_ds.T, global_query, preferred_element_type=jnp.float32)
    value_total = value_acc.reshape(LENGTH, HD) + jnp.dot(global_probs.astype(jnp.bfloat16).T, global_grad, preferred_element_type=jnp.float32)
    query_total = query_regular.reshape(LENGTH, HD)
    query_total = query_total.at[:BLOCK].set(global_dq[:BLOCK]).at[LENGTH - BLOCK:].set(global_dq[BLOCK:])
    lse_rows = row_lse.reshape(LENGTH)
    lse_rows = lse_rows.at[:BLOCK].set(global_lse[:BLOCK]).at[LENGTH - BLOCK:].set(global_lse[BLOCK:])
    sink_term = -jnp.sum(jnp.exp(sink_one - lse_rows) * row_delta)
    return (attention, query_total.astype(jnp.bfloat16), key_total.astype(jnp.bfloat16), value_total.astype(jnp.bfloat16), sink_term)

def to_heads(matrix):
    return matrix.reshape(LENGTH, HEADS, HD).transpose(1, 0, 2)

def from_heads(tensor):
    return tensor.transpose(1, 0, 2).reshape(LENGTH, HEADS * HD)

def reference(queries, key_rows, value_rows, sink_logits, partner, block_pick, out_grad):

    def per_doc(items):
        query_doc, key_doc, value_doc, grad_doc, pick_doc = items

        def per_head(head_items):
            query_one, key_one, value_one, grad_one, sink_one = head_items
            return head_pass(query_one, key_one, value_one, grad_one, sink_one, pick_doc, partner)
        results = lax.map(per_head, (to_heads(query_doc), to_heads(key_doc), to_heads(value_doc), to_heads(grad_doc), sink_logits))
        return (from_heads(results[0]), from_heads(results[1]), from_heads(results[2]), from_heads(results[3]), results[4])
    outputs = lax.map(per_doc, (queries, key_rows, value_rows, out_grad, block_pick))
    sink_grad = lax.optimization_barrier(jnp.sum(outputs[4], axis=0)) / math.sqrt(DOCS * LENGTH)
    return (outputs[0], outputs[1], outputs[2], outputs[3], sink_grad)
```

```python
import functools
import math

import jax
import jax.numpy as jnp
from jax import lax
from jax.experimental import pallas as pl
from jax.experimental.pallas import tpu as pltpu
from jax.sharding import PartitionSpec as P

HD = 128
BLOCK = 128
ROUNDS = 3
SCALE = HD ** (-0.5)
MESH = pl.DeviceIdType.MESH
F32 = jnp.float32
BF16 = jnp.bfloat16


def mm(a, b, ca, cb):
    return lax.dot_general(a, b, (((ca,), (cb,)), ((), ())), preferred_element_type=F32)


def greet(n, bit_count, me):
    barrier = pltpu.get_barrier_semaphore()
    for bit in range(bit_count):
        mask = 2**bit
        other = me + mask * (1 - 2 * ((me // mask) % 2))
        pl.semaphore_signal(barrier, inc=1, device_id={"ctx": other}, device_id_type=MESH)
    for off in (-2, -1, 1, 2):
        other = me + off

        @pl.when((other >= 0) & (other < n))
        def _():
            pl.semaphore_signal(barrier, inc=1, device_id={"ctx": other}, device_id_type=MESH)

    inside = [((me + off >= 0) & (me + off < n)).astype(jnp.int32) for off in (-2, -1, 1, 2)]
    pl.semaphore_wait(barrier, bit_count + sum(inside))


def remote(src, dst, send, recv, target):
    return pltpu.make_async_remote_copy(
        src_ref=src,
        dst_ref=dst,
        send_sem=send,
        recv_sem=recv,
        device_id={"ctx": target},
        device_id_type=MESH,
    )


def exchange_sides(n, bit_count, me, lo_src, hi_src, lo_dst, hi_dst, bit_src, bit_dst, sems):
    ws, wr, bs, br = sems

    def lower(kv):
        return remote(lo_src(kv), hi_dst(kv), ws.at[0, kv], wr.at[1, kv], me - 1)

    def upper(kv):
        return remote(hi_src(kv), lo_dst(kv), ws.at[1, kv], wr.at[0, kv], me + 1)

    def bit_copy(bit, kv):
        mask = 2**bit
        other = me + mask * (1 - 2 * ((me // mask) % 2))
        return remote(bit_src(bit, kv), bit_dst(bit, kv), bs.at[bit, kv], br.at[bit, kv], other)

    def start():
        for kv in range(2):

            @pl.when(me > 0)
            def _():
                lower(kv).start()

            @pl.when(me < n - 1)
            def _():
                upper(kv).start()

        for bit in reversed(range(bit_count)):
            for kv in range(2):
                bit_copy(bit, kv).start()

    def wait():
        for kv in range(2):

            @pl.when(me > 0)
            def _():
                lower(kv).wait_send()
                upper(kv).wait_recv()

            @pl.when(me < n - 1)
            def _():
                upper(kv).wait_send()
                lower(kv).wait_recv()

        for bit in range(bit_count):
            for kv in range(2):
                bit_copy(bit, kv).wait()

    return start, wait


def gather_kernel(
    n, bit_count, q, k, v, g, glob, win, bits, mate_s, next_s, glob_r, ws, wr, bs, br, local_s
):
    me = lax.axis_index("ctx")
    side = me % 2
    tokens = q.shape[1]
    mate = me + 1 - 2 * side
    nxt = me + 2 - 4 * side
    source = side * (n - 1)
    has_next = (nxt >= 0) & (nxt < n)
    pair = (k, v)
    greet(n, bit_count, me)

    start, wait = exchange_sides(
        n,
        bit_count,
        me,
        lambda kv: pair[kv].at[0, pl.ds(0, BLOCK)],
        lambda kv: pair[kv].at[0, pl.ds(tokens - BLOCK, BLOCK)],
        lambda kv: win.at[0, kv],
        lambda kv: win.at[1, kv],
        lambda bit, kv: pair[kv].at[0],
        lambda bit, kv: bits.at[bit, kv],
        (ws, wr, bs, br),
    )
    first_row = side * (tokens - BLOCK)

    def own_copy(j):
        ref = (q, k, v, g)[j]
        return pltpu.make_async_copy(
            ref.at[0, pl.ds(pl.multiple_of(first_row, BLOCK), BLOCK)], glob.at[side, j], local_s.at[j]
        )

    def to_mate(j, s):
        return remote(glob.at[s, j], glob.at[s, j], mate_s.at[j], glob_r.at[s, j], mate)

    def to_next(j):
        return remote(glob.at[side, j], glob.at[side, j], next_s.at[j], glob_r.at[side, j], nxt)

    order = (0, 3, 1, 2)
    is_source = me == source

    @pl.when(is_source)
    def _():
        for j in order:
            own_copy(j).start()
        for j in order:
            own_copy(j).wait()
            to_mate(j, side).start()
            to_next(j).start()

    start()

    @pl.when(jnp.logical_not(is_source))
    def _():
        for j in order:
            to_next(j).wait_recv()
            to_mate(j, side).start()

            @pl.when(has_next)
            def _():
                to_next(j).start()

    for j in order:
        to_mate(j, side).wait_send()

        @pl.when(has_next)
        def _():
            to_next(j).wait_send()

        to_mate(j, 1 - side).wait_recv()
    wait()


def return_kernel(
    n,
    bit_count,
    red,
    dwin,
    dbits,
    red_out,
    rwin,
    rbits,
    mate_buf,
    chain_buf,
    mate_s,
    mate_r,
    next_s,
    chain_r,
    ws,
    wr,
    bs,
    br,
):
    me = lax.axis_index("ctx")
    side = me % 2
    mate = me + 1 - 2 * side
    nxt = me - 2 + 4 * side
    prv = me + 2 - 4 * side
    has_next = (nxt >= 0) & (nxt < n)
    has_prev = (prv >= 0) & (prv < n)
    greet(n, bit_count, me)

    start, wait = exchange_sides(
        n,
        bit_count,
        me,
        lambda kv: dwin.at[0, kv],
        lambda kv: dwin.at[1, kv],
        lambda kv: rwin.at[0, kv],
        lambda kv: rwin.at[1, kv],
        lambda bit, kv: dbits.at[bit, kv],
        lambda bit, kv: rbits.at[bit, kv],
        (ws, wr, bs, br),
    )

    def to_mate(j):
        return remote(red.at[1 - side, j], mate_buf.at[j], mate_s.at[j], mate_r.at[j], mate)

    def to_next(j):
        return remote(red_out.at[j], chain_buf.at[j], next_s.at[j], chain_r.at[j], nxt)

    for j in range(4):
        to_mate(j).start()
    start()
    for j in range(4):
        to_mate(j).wait_recv()
        red_out[j] = (red[side, j].astype(F32) + mate_buf[j].astype(F32)).astype(BF16)

        @pl.when(has_prev)
        def _():
            to_next(j).wait_recv()
            total = red[side, j].astype(F32) + mate_buf[j].astype(F32) + chain_buf[j].astype(F32)
            red_out[j] = total.astype(BF16)

        @pl.when(has_next)
        def _():
            to_next(j).start()

    for j in range(4):
        to_mate(j).wait_send()

        @pl.when(has_next)
        def _():
            to_next(j).wait_send()

    wait()


def stats_kernel(glob, k, v, stats):
    gq = jnp.concatenate([glob[0, 0], glob[1, 0]], axis=0)
    gg = jnp.concatenate([glob[0, 3], glob[1, 3]], axis=0)
    s = mm(k[0], gq, 1, 1) * SCALE
    top = jnp.max(s, axis=0, keepdims=True)
    expo = jnp.exp(s - top)
    dp = mm(v[0], gg, 1, 1)
    stats[0, 0:1, :] = top
    stats[0, 1:2, :] = jnp.sum(expo, axis=0, keepdims=True)
    stats[0, 2:3, :] = jnp.sum(expo.astype(BF16).astype(F32) * dp, axis=0, keepdims=True)


def regular_kernel(
    info,
    sink_ref,
    q,
    k,
    v,
    g,
    win,
    glob,
    r0,
    r1,
    r2,
    att,
    dq,
    own,
    dwin,
    dglob,
    dbits,
    sink_out,
    racc,
):
    head = pl.program_id(0)
    is_first = info[6] == 1
    is_last = info[7] == 1
    sink = sink_ref[head]
    tokens = q.shape[1]
    count = tokens // BLOCK
    randoms = (r0, r1, r2)
    ext, shared = [], []
    for kv, ref in enumerate((k, v)):
        lo = jnp.where(is_first, jnp.zeros((BLOCK, HD), BF16), win[0, kv])
        hi = jnp.where(is_last, jnp.zeros((BLOCK, HD), BF16), win[1, kv])
        ext.append([lo] + [ref[0, i * BLOCK : (i + 1) * BLOCK] for i in range(count)] + [hi])
        shared.append([glob[0, 1 + kv], glob[1, 1 + kv]] + [r[0, kv] for r in randoms])
    slots = 5 + ROUNDS
    col = lax.broadcasted_iota(jnp.int32, (BLOCK, slots * BLOCK), 1)
    ext_grad = [[None] * (count + 2), [None] * (count + 2)]
    shared_grad = [None, None]
    sink_sum = jnp.zeros((1, 1), F32)
    for b in range(count):
        keys = jnp.concatenate(ext[0][b : b + 3] + shared[0], axis=0)
        vals = jnp.concatenate(ext[1][b : b + 3] + shared[1], axis=0)
        rows = slice(b * BLOCK, (b + 1) * BLOCK)
        qb, gb = q[0, rows], g[0, rows]
        s = mm(qb, keys, 1, 1) * SCALE
        if b == 1:
            s = jnp.where(is_first & (col < BLOCK), -jnp.inf, s)
        if b == count - 2:
            s = jnp.where(is_last & (col >= 2 * BLOCK) & (col < 3 * BLOCK), -jnp.inf, s)
        top = jnp.maximum(jnp.max(s, axis=1, keepdims=True), sink)
        expo = jnp.exp(s - top)
        at_sink = jnp.exp(sink - top)
        total = at_sink + jnp.sum(expo, axis=1, keepdims=True)
        inv = 1.0 / total
        out = (mm(expo.astype(BF16), vals, 1, 0) * inv).astype(BF16)
        att[rows, :] = out
        delta = jnp.sum(gb.astype(F32) * out.astype(F32), axis=1, keepdims=True)
        keep = None
        if b == 0:
            keep = jnp.logical_not(is_first)
        if b == count - 1:
            last_ok = jnp.logical_not(is_last)
            keep = last_ok if keep is None else keep & last_ok
        if keep is not None:
            inv = jnp.where(keep, inv, 0.0)
        probs = expo * inv
        dp = mm(gb, vals, 1, 1)
        ds = (probs * (dp - delta)).astype(BF16)
        ph = probs.astype(BF16)
        sink_sum = sink_sum - jnp.sum(at_sink * inv * delta, axis=0, keepdims=True)
        dq[rows, :] = (mm(ds, keys, 1, 0) * SCALE).astype(BF16)
        for kv, full in enumerate((mm(ds, qb, 0, 0) * SCALE, mm(ph, gb, 0, 0))):
            for i in range(3):
                part = full[i * BLOCK : (i + 1) * BLOCK]
                old = ext_grad[kv][b + i]
                ext_grad[kv][b + i] = part if old is None else old + part
            rest = full[3 * BLOCK :]
            shared_grad[kv] = rest if shared_grad[kv] is None else shared_grad[kv] + rest
    racc[...] = jnp.zeros_like(racc)
    for kv in range(2):
        dwin[0, kv] = ext_grad[kv][0].astype(BF16)
        dwin[1, kv] = ext_grad[kv][count + 1].astype(BF16)
        for i in range(count):
            own[kv, i * BLOCK : (i + 1) * BLOCK, :] = ext_grad[kv][i + 1]
        dglob[0, kv] = shared_grad[kv][:BLOCK].astype(BF16)
        dglob[1, kv] = shared_grad[kv][BLOCK : 2 * BLOCK].astype(BF16)
        for r in range(ROUNDS):
            at = pl.ds(pl.multiple_of(info[ROUNDS + r] * BLOCK, BLOCK), BLOCK)
            racc[info[r], kv, at, :] += shared_grad[kv][(2 + r) * BLOCK : (3 + r) * BLOCK]
    dbits[...] = racc[...].astype(BF16)
    sink_out[0] = jnp.broadcast_to(sink_sum, (8, 128))


def global_kernel(info, sink_ref, stats, glob, k, v, own, dglob, sink_in, own_out, red, sink_out):
    head = pl.program_id(0)
    sink = sink_ref[head]
    is_first = info[6] == 1
    is_last = info[7] == 1
    peers = stats.shape[0]
    gq = jnp.concatenate([glob[0, 0], glob[1, 0]], axis=0)
    gg = jnp.concatenate([glob[0, 3], glob[1, 3]], axis=0)
    tops = [stats[c, 0, 0:1, :] for c in range(peers)]
    top = functools.reduce(jnp.maximum, tops)
    top = jnp.maximum(top, sink)
    at_sink = jnp.exp(sink - top)
    total = at_sink
    delta = jnp.zeros_like(top)
    for c in range(peers):
        ratio = jnp.exp(tops[c] - top)
        total = total + stats[c, 0, 1:2, :] * ratio
        delta = delta + stats[c, 0, 2:3, :] * ratio
    inv = 1.0 / total
    delta = delta * inv
    s = mm(k[0], gq, 1, 1) * SCALE
    probs = jnp.exp(s - top) * inv
    dp = mm(v[0], gg, 1, 1)
    ds = (probs * (dp - delta)).astype(BF16)
    ph = probs.astype(BF16)
    own_out[0] = own[0] + mm(ds, gq, 1, 0) * SCALE
    own_out[1] = own[1] + mm(ph, gg, 1, 0)
    out = mm(ph, v[0], 0, 0).astype(BF16)
    gdq = (mm(ds, k[0], 0, 0) * SCALE).astype(BF16)
    for s_ in range(2):
        rows = slice(s_ * BLOCK, (s_ + 1) * BLOCK)
        red[s_, 0] = out[rows]
        red[s_, 1] = gdq[rows]
        red[s_, 2] = dglob[s_, 0]
        red[s_, 3] = dglob[s_, 1]
    terms = at_sink * inv * delta
    lane = lax.broadcasted_iota(jnp.int32, terms.shape, 1)
    mine = (is_first & (lane < BLOCK)) | (is_last & (lane >= BLOCK))
    part = jnp.sum(jnp.where(mine, terms, 0.0), axis=1, keepdims=True)
    sink_out[0] = sink_in[0] - jnp.broadcast_to(part, (8, 128))


def final_kernel(bit_count, info, att, dq, own, red, rwin, rbits, att_o, dq_o, dk_o, dv_o):
    is_first = info[6] == 1
    is_last = info[7] == 1
    tokens = att.shape[0]
    count = tokens // BLOCK
    for b in range(count):
        rows = slice(b * BLOCK, (b + 1) * BLOCK)
        a, d = att[rows, :], dq[rows, :]
        grads = [own[kv, rows, :] for kv in range(2)]
        for bit in range(bit_count):
            grads = [grads[kv] + rbits[bit, kv, rows, :].astype(F32) for kv in range(2)]
        for edge, here, side in ((0, is_first, 0), (count - 1, is_last, 1)):
            if b == edge:
                a = jnp.where(here, red[0], a)
                d = jnp.where(here, red[1], d)
                for kv in range(2):
                    grads[kv] = grads[kv] + jnp.where(here, red[2 + kv], rwin[side, kv]).astype(F32)
        att_o[0, rows, :] = a
        dq_o[0, rows, :] = d
        dk_o[0, rows, :] = grads[0].astype(BF16)
        dv_o[0, rows, :] = grads[1].astype(BF16)


def body(queries, key_rows, value_rows, sink_logits, partner, block_pick, out_grad):
    _, tokens, width = queries.shape
    heads = width // HD
    n = lax.axis_size("ctx")
    bit_count = n.bit_length() - 1
    me = lax.axis_index("ctx")
    any_spec = pl.BlockSpec(memory_space=pl.ANY)
    dma = pltpu.SemaphoreType.DMA
    masks = partner[:, 0]
    bit_of = sum(b * (jnp.right_shift(masks, b) & 1) for b in range(bit_count))
    place = jnp.bitwise_xor(me, masks)
    match = jnp.arange(n)[None, :] == place[:, None]
    del match
    wanted = block_pick[0, :, :]
    picked = jnp.sum(jnp.where(jnp.arange(n)[None, :] == me, wanted, 0), axis=1)
    flags = jnp.stack([me == 0, me == n - 1]).astype(jnp.int32)
    info = jnp.concatenate([bit_of, picked, flags]).astype(jnp.int32)
    side_sems = [dma((2, 2)), dma((2, 2)), dma((bit_count, 2)), dma((bit_count, 2))]

    def shape(dims, dtype=BF16):
        return jax.ShapeDtypeStruct(dims, dtype)

    glob, win, bits = pl.pallas_call(
        functools.partial(gather_kernel, n, bit_count),
        out_shape=(
            shape((2, 4, BLOCK, width)),
            shape((2, 2, BLOCK, width)),
            shape((bit_count, 2, tokens, width)),
        ),
        in_specs=[any_spec] * 4,
        out_specs=(any_spec,) * 3,
        scratch_shapes=[dma((4,)), dma((4,)), dma((2, 4))] + side_sems + [dma((4,))],
        compiler_params=pltpu.CompilerParams(collective_id=0, has_side_effects=True),
        name="gather_blocks",
    )(queries, key_rows, value_rows, out_grad)

    smem = pl.BlockSpec(memory_space=pltpu.SMEM)
    rows_in = pl.BlockSpec((1, tokens, HD), lambda h, *_: (0, 0, h))
    rows_out = pl.BlockSpec((tokens, HD), lambda h, *_: (0, h))
    own_spec = pl.BlockSpec((2, tokens, HD), lambda h, *_: (0, 0, h))
    glob_spec = pl.BlockSpec((2, 4, BLOCK, HD), lambda h, *_: (0, 0, 0, h))
    win_spec = pl.BlockSpec((2, 2, BLOCK, HD), lambda h, *_: (0, 0, 0, h))
    bits_spec = pl.BlockSpec((bit_count, 2, tokens, HD), lambda h, *_: (0, 0, 0, h))
    sink_spec = pl.BlockSpec((1, 8, 128), lambda h, *_: (h, 0, 0))
    stat_spec = pl.BlockSpec((1, 3, 2 * BLOCK), lambda h, *_: (h, 0, 0))
    params = pltpu.CompilerParams(vmem_limit_bytes=40 * 1024 * 1024)

    stats = pl.pallas_call(
        stats_kernel,
        grid=(heads,),
        in_specs=[glob_spec, rows_in, rows_in],
        out_specs=stat_spec,
        out_shape=shape((heads, 3, 2 * BLOCK), F32),
        compiler_params=params,
        name="global_stats",
    )(glob, key_rows, value_rows)
    all_stats = lax.all_gather(stats, "ctx")

    def random_spec(r):
        return pl.BlockSpec(
            (1, 2, BLOCK, HD), lambda h, info: (info[r], 0, info[ROUNDS + r], h)
        )

    att, dq, own, dwin, dglob, dbits, sink_part = pl.pallas_call(
        regular_kernel,
        grid_spec=pltpu.PrefetchScalarGridSpec(
            num_scalar_prefetch=1,
            grid=(heads,),
            in_specs=[smem, rows_in, rows_in, rows_in, rows_in, win_spec, glob_spec]
            + [random_spec(r) for r in range(ROUNDS)],
            out_specs=(rows_out, rows_out, own_spec, win_spec, win_spec, bits_spec, sink_spec),
            scratch_shapes=[pltpu.VMEM((bit_count, 2, tokens, HD), F32)],
        ),
        out_shape=(
            shape((tokens, width)),
            shape((tokens, width)),
            shape((2, tokens, width), F32),
            shape((2, 2, BLOCK, width)),
            shape((2, 2, BLOCK, width)),
            shape((bit_count, 2, tokens, width)),
            shape((heads, 8, 128), F32),
        ),
        compiler_params=params,
        cost_estimate=pl.CostEstimate(
            flops=4 * 10**9, bytes_accessed=2 * 10**7, transcendentals=3 * 10**6
        ),
        name="regular_rows",
    )(
        info,
        sink_logits,
        queries,
        key_rows,
        value_rows,
        out_grad,
        win,
        glob,
        bits,
        bits,
        bits,
    )

    own, red, sink_part = pl.pallas_call(
        global_kernel,
        grid_spec=pltpu.PrefetchScalarGridSpec(
            num_scalar_prefetch=1,
            grid=(heads,),
            in_specs=[
                smem,
                pl.BlockSpec((n, 1, 3, 2 * BLOCK), lambda h, *_: (0, h, 0, 0)),
                glob_spec,
                rows_in,
                rows_in,
                own_spec,
                win_spec,
                sink_spec,
            ],
            out_specs=(own_spec, glob_spec, sink_spec),
        ),
        out_shape=(
            shape((2, tokens, width), F32),
            shape((2, 4, BLOCK, width)),
            shape((heads, 8, 128), F32),
        ),
        compiler_params=params,
        name="global_rows",
    )(info, sink_logits, all_stats, glob, key_rows, value_rows, own, dglob, sink_part)

    sink_total = lax.psum(sink_part[:, 0, 0], ("dp", "ctx"))
    sink_grad = sink_total / math.sqrt(lax.axis_size("dp") * n * tokens)

    vmem = pl.BlockSpec(memory_space=pltpu.VMEM)
    red, rwin, rbits = pl.pallas_call(
        functools.partial(return_kernel, n, bit_count),
        out_shape=(
            shape((4, BLOCK, width)),
            shape((2, 2, BLOCK, width)),
            shape((bit_count, 2, tokens, width)),
        ),
        in_specs=[vmem, any_spec, any_spec],
        out_specs=(vmem, any_spec, any_spec),
        scratch_shapes=[
            pltpu.VMEM((4, BLOCK, width), BF16),
            pltpu.VMEM((4, BLOCK, width), BF16),
            dma((4,)),
            dma((4,)),
            dma((4,)),
            dma((4,)),
        ]
        + side_sems,
        compiler_params=pltpu.CompilerParams(
            collective_id=1, has_side_effects=True, vmem_limit_bytes=40 * 1024 * 1024
        ),
        name="return_blocks",
    )(red, dwin, dbits)

    final_spec = pl.BlockSpec((1, tokens, HD), lambda h, *_: (0, 0, h))
    outs = pl.pallas_call(
        functools.partial(final_kernel, bit_count),
        grid_spec=pltpu.PrefetchScalarGridSpec(
            num_scalar_prefetch=1,
            grid=(heads,),
            in_specs=[
                rows_out,
                rows_out,
                own_spec,
                pl.BlockSpec((4, BLOCK, HD), lambda h, *_: (0, 0, h)),
                win_spec,
                bits_spec,
            ],
            out_specs=(final_spec,) * 4,
        ),
        out_shape=(shape((1, tokens, width)),) * 4,
        compiler_params=params,
        name="add_up",
    )(info, att, dq, own, red, rwin, rbits)
    return (*outs, sink_grad)


def solution(mesh):
    rows = P("dp", "ctx", "head")
    return jax.shard_map(
        body,
        mesh=mesh,
        in_specs=(rows, rows, rows, P("head"), P(), P("dp", None, None), rows),
        out_specs=(rows, rows, rows, rows, P("head")),
        check_vma=False,
    )
```

```python
import functools
import math

import jax
import jax.numpy as jnp
from jax import lax
from jax.experimental import pallas as pl
from jax.experimental.pallas import tpu as pltpu
from jax.sharding import PartitionSpec as P

HD = 128
BLOCK = 128
ROUNDS = 3
VARIED = 2
SCALE = HD ** (-0.5)
MESH = pl.DeviceIdType.MESH
F32 = jnp.float32
BF16 = jnp.bfloat16


def mm(a, b, ca, cb):
    return lax.dot_general(a, b, (((ca,), (cb,)), ((), ())), preferred_element_type=F32)


def flipped(place, bit):
    mask = 2**bit
    return place + mask * (1 - 2 * ((place // mask) % 2))


def greet(n, bit_count, me, doc_bits=0):
    barrier = pltpu.get_barrier_semaphore()
    for bit in range(bit_count):
        other = flipped(me, bit)
        pl.semaphore_signal(barrier, inc=1, device_id={"ctx": other}, device_id_type=MESH)
    for bit in range(doc_bits):
        other = flipped(lax.axis_index("dp"), bit)
        pl.semaphore_signal(barrier, inc=1, device_id={"dp": other}, device_id_type=MESH)
    for off in (-2, -1, 1, 2):
        other = me + off

        @pl.when((other >= 0) & (other < n))
        def _():
            pl.semaphore_signal(barrier, inc=1, device_id={"ctx": other}, device_id_type=MESH)

    inside = [((me + off >= 0) & (me + off < n)).astype(jnp.int32) for off in (-2, -1, 1, 2)]
    pl.semaphore_wait(barrier, bit_count + doc_bits + sum(inside))


def remote(src, dst, send, recv, target, axis="ctx"):
    return pltpu.make_async_remote_copy(
        src_ref=src,
        dst_ref=dst,
        send_sem=send,
        recv_sem=recv,
        device_id={axis: target},
        device_id_type=MESH,
    )


def exchange_sides(n, bits_used, me, lo_src, hi_src, lo_dst, hi_dst, bit_src, bit_dst, sems):
    ws, wr, bs, br = sems

    def lower(kv):
        return remote(lo_src(kv), hi_dst(kv), ws.at[0, kv], wr.at[1, kv], me - 1)

    def upper(kv):
        return remote(hi_src(kv), lo_dst(kv), ws.at[1, kv], wr.at[0, kv], me + 1)

    def bit_copy(bit, kv):
        other = flipped(me, bit)
        return remote(bit_src(bit, kv), bit_dst(bit, kv), bs.at[bit, kv], br.at[bit, kv], other)

    def start():
        for kv in range(2):

            @pl.when(me > 0)
            def _():
                lower(kv).start()

            @pl.when(me < n - 1)
            def _():
                upper(kv).start()

        for bit in reversed(bits_used):
            for kv in range(2):
                bit_copy(bit, kv).start()

    def wait():
        for kv in range(2):

            @pl.when(me > 0)
            def _():
                lower(kv).wait_send()
                upper(kv).wait_recv()

            @pl.when(me < n - 1)
            def _():
                upper(kv).wait_send()
                lower(kv).wait_recv()

        for bit in bits_used:
            for kv in range(2):
                bit_copy(bit, kv).wait()

    return start, wait


def used_bits(bit_count, mode):
    return [bit for bit in range(bit_count) if bit != VARIED or mode > 0]


def part_of(ref, bit, kv, mode):
    if mode == 1 and bit == VARIED:
        return ref.at[bit, kv, pl.ds(0, BLOCK)]
    return ref.at[bit, kv]


def gather_kernel(n, bit_count, mode, *refs):
    q, k, v, g = refs[:4]
    packed = refs[4] if mode == 1 else None
    glob, win, bits, stats = refs[-16:-12]
    own_stats, got_stats, mate_s, next_s, glob_r, ws, wr, bs, br, local_s = refs[-12:-2]
    stat_s, stat_r = refs[-2:]
    me = lax.axis_index("ctx")
    side = me % 2
    tokens = q.shape[1]
    mate = me + 1 - 2 * side
    nxt = me + 2 - 4 * side
    source = side * (n - 1)
    has_next = (nxt >= 0) & (nxt < n)
    pair = (k, v)
    greet(n, bit_count, me)

    start, wait = exchange_sides(
        n,
        used_bits(bit_count, mode),
        me,
        lambda kv: pair[kv].at[0, pl.ds(0, BLOCK)],
        lambda kv: pair[kv].at[0, pl.ds(tokens - BLOCK, BLOCK)],
        lambda kv: win.at[0, kv],
        lambda kv: win.at[1, kv],
        lambda bit, kv: packed.at[kv] if mode == 1 and bit == VARIED else pair[kv].at[0],
        lambda bit, kv: part_of(bits, bit, kv, mode),
        (ws, wr, bs, br),
    )
    first_row = side * (tokens - BLOCK)

    def own_copy(j):
        ref = (q, k, v, g)[j]
        return pltpu.make_async_copy(
            ref.at[0, pl.ds(pl.multiple_of(first_row, BLOCK), BLOCK)], glob.at[side, j], local_s.at[j]
        )

    def to_mate(j, s):
        return remote(glob.at[s, j], glob.at[s, j], mate_s.at[j], glob_r.at[s, j], mate)

    def to_next(j):
        return remote(glob.at[side, j], glob.at[side, j], next_s.at[j], glob_r.at[side, j], nxt)

    order = (0, 3, 1, 2)
    is_source = me == source

    @pl.when(is_source)
    def _():
        for j in order:
            own_copy(j).start()
        for j in order:
            own_copy(j).wait()
            to_mate(j, side).start()
            to_next(j).start()

    start()

    @pl.when(jnp.logical_not(is_source))
    def _():
        for j in order:
            to_next(j).wait_recv()
            to_mate(j, side).start()

            @pl.when(has_next)
            def _():
                to_next(j).start()

    for j in order:
        to_mate(j, side).wait_send()

        @pl.when(has_next)
        def _():
            to_next(j).wait_send()

        to_mate(j, 1 - side).wait_recv()

    for h in range(q.shape[2] // HD):
        cols = slice(h * HD, (h + 1) * HD)
        gq = jnp.concatenate([glob[0, 0, :, cols], glob[1, 0, :, cols]], axis=0)
        gg = jnp.concatenate([glob[0, 3, :, cols], glob[1, 3, :, cols]], axis=0)
        s = mm(k[0, :, cols], gq, 1, 1) * SCALE
        top = jnp.max(s, axis=0, keepdims=True)
        expo = jnp.exp(s - top)
        dp = mm(v[0, :, cols], gg, 1, 1)
        own_stats[0, 0, h : h + 1, :] = top
        own_stats[0, 1, h : h + 1, :] = jnp.sum(expo, axis=0, keepdims=True)
        own_stats[0, 2, h : h + 1, :] = jnp.sum(
            expo.astype(BF16).astype(F32) * dp, axis=0, keepdims=True
        )

    def swap(bit):
        return remote(
            own_stats.at[bit], got_stats.at[bit], stat_s.at[bit], stat_r.at[bit], flipped(me, bit)
        )

    for bit in range(bit_count):
        swap(bit).start()
        swap(bit).wait_recv()
        top = jnp.maximum(own_stats[bit, 0], got_stats[bit, 0])
        mine = jnp.exp(own_stats[bit, 0] - top)
        other = jnp.exp(got_stats[bit, 0] - top)
        merged = [top] + [own_stats[bit, i] * mine + got_stats[bit, i] * other for i in (1, 2)]
        for i in range(3):
            if bit < bit_count - 1:
                own_stats[bit + 1, i] = merged[i]
            else:
                stats[i] = merged[i]
    for bit in range(bit_count):
        swap(bit).wait_send()
    wait()


def return_kernel(
    n,
    bit_count,
    doc_bits,
    mode,
    red,
    dwin,
    dbits,
    sink_in,
    red_out,
    rwin,
    rbits,
    sink_out,
    sink_send,
    sink_recv,
    mate_buf,
    chain_buf,
    mate_s,
    mate_r,
    next_s,
    chain_r,
    ws,
    wr,
    bs,
    br,
    sink_s,
    sink_r,
):
    me = lax.axis_index("ctx")
    side = me % 2
    mate = me + 1 - 2 * side
    nxt = me - 2 + 4 * side
    prv = me + 2 - 4 * side
    has_next = (nxt >= 0) & (nxt < n)
    has_prev = (prv >= 0) & (prv < n)
    greet(n, bit_count, me, doc_bits)

    start, wait = exchange_sides(
        n,
        used_bits(bit_count, mode),
        me,
        lambda kv: dwin.at[0, kv],
        lambda kv: dwin.at[1, kv],
        lambda kv: rwin.at[0, kv],
        lambda kv: rwin.at[1, kv],
        lambda bit, kv: part_of(dbits, bit, kv, mode),
        lambda bit, kv: part_of(rbits, bit, kv, mode),
        (ws, wr, bs, br),
    )

    def to_mate(j):
        return remote(red.at[1 - side, j], mate_buf.at[j], mate_s.at[j], mate_r.at[j], mate)

    def to_next(j):
        return remote(red_out.at[j], chain_buf.at[j], next_s.at[j], chain_r.at[j], nxt)

    for j in range(4):
        to_mate(j).start()
    start()
    for j in range(4):
        to_mate(j).wait_recv()
        red_out[j] = (red[side, j].astype(F32) + mate_buf[j].astype(F32)).astype(BF16)

        @pl.when(has_prev)
        def _():
            to_next(j).wait_recv()
            total = red[side, j].astype(F32) + mate_buf[j].astype(F32) + chain_buf[j].astype(F32)
            red_out[j] = total.astype(BF16)

        @pl.when(has_next)
        def _():
            to_next(j).start()

    for j in range(4):
        to_mate(j).wait_send()

        @pl.when(has_next)
        def _():
            to_next(j).wait_send()

    steps = bit_count + doc_bits

    def swap(i):
        if i < doc_bits:
            axis, target = "dp", flipped(lax.axis_index("dp"), i)
        else:
            axis, target = "ctx", flipped(me, i - doc_bits)
        return remote(sink_send.at[i], sink_recv.at[i], sink_s.at[i], sink_r.at[i], target, axis)

    sink_send[0] = sink_in[...]
    for i in range(steps):
        swap(i).start()
        swap(i).wait_recv()
        total = sink_send[i] + sink_recv[i]
        if i < steps - 1:
            sink_send[i + 1] = total
        else:
            sink_out[...] = total
    for i in range(steps):
        swap(i).wait_send()
    wait()


def regular_kernel(
    info,
    sink_ref,
    q,
    k,
    v,
    g,
    win,
    glob,
    r0,
    r1,
    r2,
    att,
    dq,
    own,
    dwin,
    dglob,
    dbits,
    sink_out,
    racc,
):
    head = pl.program_id(0)
    is_first = info[6] == 1
    is_last = info[7] == 1
    sink = sink_ref[head]
    tokens = q.shape[1]
    count = tokens // BLOCK
    randoms = (r0, r1, r2)
    ext, shared = [], []
    for kv, ref in enumerate((k, v)):
        lo = jnp.where(is_first, jnp.zeros((BLOCK, HD), BF16), win[0, kv])
        hi = jnp.where(is_last, jnp.zeros((BLOCK, HD), BF16), win[1, kv])
        ext.append([lo] + [ref[0, i * BLOCK : (i + 1) * BLOCK] for i in range(count)] + [hi])
        shared.append([glob[0, 1 + kv], glob[1, 1 + kv]] + [r[0, kv] for r in randoms])
    slots = 5 + ROUNDS
    col = lax.broadcasted_iota(jnp.int32, (BLOCK, slots * BLOCK), 1)
    ext_grad = [[None] * (count + 2), [None] * (count + 2)]
    shared_grad = [None, None]
    sink_sum = jnp.zeros((1, 1), F32)
    for b in range(count):
        keys = jnp.concatenate(ext[0][b : b + 3] + shared[0], axis=0)
        vals = jnp.concatenate(ext[1][b : b + 3] + shared[1], axis=0)
        rows = slice(b * BLOCK, (b + 1) * BLOCK)
        qb, gb = q[0, rows], g[0, rows]
        s = mm(qb, keys, 1, 1) * SCALE
        if b == 1:
            s = jnp.where(is_first & (col < BLOCK), -jnp.inf, s)
        if b == count - 2:
            s = jnp.where(is_last & (col >= 2 * BLOCK) & (col < 3 * BLOCK), -jnp.inf, s)
        top = jnp.maximum(jnp.max(s, axis=1, keepdims=True), sink)
        expo = jnp.exp(s - top)
        at_sink = jnp.exp(sink - top)
        total = at_sink + jnp.sum(expo, axis=1, keepdims=True)
        inv = 1.0 / total
        out = (mm(expo.astype(BF16), vals, 1, 0) * inv).astype(BF16)
        att[rows, :] = out
        delta = jnp.sum(gb.astype(F32) * out.astype(F32), axis=1, keepdims=True)
        keep = None
        if b == 0:
            keep = jnp.logical_not(is_first)
        if b == count - 1:
            last_ok = jnp.logical_not(is_last)
            keep = last_ok if keep is None else keep & last_ok
        if keep is not None:
            inv = jnp.where(keep, inv, 0.0)
        probs = expo * inv
        dp = mm(gb, vals, 1, 1)
        ds = (probs * (dp - delta)).astype(BF16)
        ph = probs.astype(BF16)
        sink_sum = sink_sum - jnp.sum(at_sink * inv * delta, axis=0, keepdims=True)
        dq[rows, :] = (mm(ds, keys, 1, 0) * SCALE).astype(BF16)
        for kv, full in enumerate((mm(ds, qb, 0, 0) * SCALE, mm(ph, gb, 0, 0))):
            for i in range(3):
                part = full[i * BLOCK : (i + 1) * BLOCK]
                old = ext_grad[kv][b + i]
                ext_grad[kv][b + i] = part if old is None else old + part
            rest = full[3 * BLOCK :]
            shared_grad[kv] = rest if shared_grad[kv] is None else shared_grad[kv] + rest
    racc[...] = jnp.zeros_like(racc)
    for kv in range(2):
        dwin[0, kv] = ext_grad[kv][0].astype(BF16)
        dwin[1, kv] = ext_grad[kv][count + 1].astype(BF16)
        for i in range(count):
            own[kv, i * BLOCK : (i + 1) * BLOCK, :] = ext_grad[kv][i + 1]
        dglob[0, kv] = shared_grad[kv][:BLOCK].astype(BF16)
        dglob[1, kv] = shared_grad[kv][BLOCK : 2 * BLOCK].astype(BF16)
        for r in range(ROUNDS):
            at = pl.ds(pl.multiple_of(info[ROUNDS + r] * BLOCK, BLOCK), BLOCK)
            racc[info[r], kv, at, :] += shared_grad[kv][(2 + r) * BLOCK : (3 + r) * BLOCK]
    dbits[...] = racc[...].astype(BF16)
    sink_out[0] = jnp.broadcast_to(sink_sum, (8, 128))


def global_kernel(info, sink_ref, stats, glob, k, v, own, dglob, sink_in, own_out, red, sink_out):
    head = pl.program_id(0)
    sink = sink_ref[head]
    is_first = info[6] == 1
    is_last = info[7] == 1
    gq = jnp.concatenate([glob[0, 0], glob[1, 0]], axis=0)
    gg = jnp.concatenate([glob[0, 3], glob[1, 3]], axis=0)
    row = pl.ds(head, 1)
    shard_top = stats[0, row, :]
    top = jnp.maximum(shard_top, sink)
    at_sink = jnp.exp(sink - top)
    ratio = jnp.exp(shard_top - top)
    inv = 1.0 / (at_sink + stats[1, row, :] * ratio)
    delta = stats[2, row, :] * ratio * inv
    s = mm(k[0], gq, 1, 1) * SCALE
    probs = jnp.exp(s - top) * inv
    dp = mm(v[0], gg, 1, 1)
    ds = (probs * (dp - delta)).astype(BF16)
    ph = probs.astype(BF16)
    own_out[0] = own[0] + mm(ds, gq, 1, 0) * SCALE
    own_out[1] = own[1] + mm(ph, gg, 1, 0)
    out = mm(ph, v[0], 0, 0).astype(BF16)
    gdq = (mm(ds, k[0], 0, 0) * SCALE).astype(BF16)
    for s_ in range(2):
        rows = slice(s_ * BLOCK, (s_ + 1) * BLOCK)
        red[s_, 0] = out[rows]
        red[s_, 1] = gdq[rows]
        red[s_, 2] = dglob[s_, 0]
        red[s_, 3] = dglob[s_, 1]
    terms = at_sink * inv * delta
    lane = lax.broadcasted_iota(jnp.int32, terms.shape, 1)
    mine = (is_first & (lane < BLOCK)) | (is_last & (lane >= BLOCK))
    part = jnp.sum(jnp.where(mine, terms, 0.0), axis=1, keepdims=True)
    sink_out[0] = sink_in[0] - jnp.broadcast_to(part, (8, 128))


def final_kernel(bit_count, info, att, dq, own, red, rwin, rbits, att_o, dq_o, dk_o, dv_o):
    is_first = info[6] == 1
    is_last = info[7] == 1
    tokens = att.shape[0]
    count = tokens // BLOCK
    for b in range(count):
        rows = slice(b * BLOCK, (b + 1) * BLOCK)
        a, d = att[rows, :], dq[rows, :]
        grads = [own[kv, rows, :] for kv in range(2)]
        for bit in range(bit_count):
            for kv in range(2):
                term = rbits[bit, kv, rows, :]
                if bit == VARIED:
                    single = (info[8] == 1) & (info[9] == b)
                    term = jnp.where(info[8] == 2, term, jnp.zeros_like(term))
                    term = jnp.where(single, rbits[bit, kv, :BLOCK, :], term)
                grads[kv] = grads[kv] + term.astype(F32)
        for edge, here, side in ((0, is_first, 0), (count - 1, is_last, 1)):
            if b == edge:
                a = jnp.where(here, red[0], a)
                d = jnp.where(here, red[1], d)
                for kv in range(2):
                    grads[kv] = grads[kv] + jnp.where(here, red[2 + kv], rwin[side, kv]).astype(F32)
        att_o[0, rows, :] = a
        dq_o[0, rows, :] = d
        dk_o[0, rows, :] = grads[0].astype(BF16)
        dv_o[0, rows, :] = grads[1].astype(BF16)


def body(queries, key_rows, value_rows, sink_logits, partner, block_pick, out_grad):
    _, tokens, width = queries.shape
    heads = width // HD
    n = lax.axis_size("ctx")
    bit_count = n.bit_length() - 1
    me = lax.axis_index("ctx")
    any_spec = pl.BlockSpec(memory_space=pl.ANY)
    dma = pltpu.SemaphoreType.DMA
    masks = partner[:, 0]
    bit_of = sum(b * (jnp.right_shift(masks, b) & 1) for b in range(bit_count))
    place = jnp.bitwise_xor(me, masks)
    ids = jnp.arange(n)[None, :]
    picked = jnp.sum(jnp.where(ids == me, block_pick[0], 0), axis=1)
    asked = jnp.sum(jnp.where(ids == place[:, None], block_pick[0], 0), axis=1)
    varied = bit_of == VARIED
    mode = jnp.minimum(jnp.sum(varied.astype(jnp.int32)), 2)
    slot = jnp.where(varied & (mode == 1), 0, picked)
    asked_block = jnp.where(mode == 1, jnp.sum(jnp.where(varied, asked, 0)), 0)
    extra = jnp.stack([(me == 0) * 1, (me == n - 1) * 1, mode, asked_block])
    info = jnp.concatenate([bit_of, slot, extra]).astype(jnp.int32)
    doc_bits = lax.axis_size("dp").bit_length() - 1
    steps = bit_count + doc_bits
    params = pltpu.CompilerParams(vmem_limit_bytes=40 * 1024 * 1024)
    vmem = pl.BlockSpec(memory_space=pltpu.VMEM)
    side_sems = [dma((2, 2)), dma((2, 2)), dma((bit_count, 2)), dma((bit_count, 2))]

    def shape(dims, dtype=BF16):
        return jax.ShapeDtypeStruct(dims, dtype)

    def gather(kind, q, k, v, g):
        args = [q, k, v, g]
        if kind == 1:
            start = (0, asked_block * BLOCK, 0)
            cut = [lax.dynamic_slice(rows, start, (1, BLOCK, width)) for rows in (k, v)]
            args.append(jnp.concatenate(cut, axis=0))
        return pl.pallas_call(
            functools.partial(gather_kernel, n, bit_count, kind),
            out_shape=(
                shape((2, 4, BLOCK, width)),
                shape((2, 2, BLOCK, width)),
                shape((bit_count, 2, tokens, width)),
                shape((3, heads, 2 * BLOCK), F32),
            ),
            in_specs=[any_spec, vmem, vmem, any_spec] + [any_spec] * (len(args) - 4),
            out_specs=(vmem, any_spec, any_spec, vmem),
            scratch_shapes=[
                pltpu.VMEM((bit_count, 3, heads, 2 * BLOCK), F32),
                pltpu.VMEM((bit_count, 3, heads, 2 * BLOCK), F32),
                dma((4,)),
                dma((4,)),
                dma((2, 4)),
            ]
            + side_sems
            + [dma((4,)), dma((bit_count,)), dma((bit_count,))],
            compiler_params=pltpu.CompilerParams(
                collective_id=kind, has_side_effects=True, vmem_limit_bytes=40 * 1024 * 1024
            ),
            name=f"gather_blocks_{kind}",
        )(*args)

    glob, win, bits, all_stats = lax.switch(
        mode,
        [functools.partial(gather, kind) for kind in range(3)],
        queries,
        key_rows,
        value_rows,
        out_grad,
    )

    smem = pl.BlockSpec(memory_space=pltpu.SMEM)
    rows_in = pl.BlockSpec((1, tokens, HD), lambda h, *_: (0, 0, h))
    rows_out = pl.BlockSpec((tokens, HD), lambda h, *_: (0, h))
    own_spec = pl.BlockSpec((2, tokens, HD), lambda h, *_: (0, 0, h))
    glob_spec = pl.BlockSpec((2, 4, BLOCK, HD), lambda h, *_: (0, 0, 0, h))
    win_spec = pl.BlockSpec((2, 2, BLOCK, HD), lambda h, *_: (0, 0, 0, h))
    bits_spec = pl.BlockSpec((bit_count, 2, tokens, HD), lambda h, *_: (0, 0, 0, h))
    sink_spec = pl.BlockSpec((1, 8, 128), lambda h, *_: (h, 0, 0))
    def random_spec(r):
        return pl.BlockSpec(
            (1, 2, BLOCK, HD), lambda h, info: (info[r], 0, info[ROUNDS + r], h)
        )

    att, dq, own, dwin, dglob, dbits, sink_part = pl.pallas_call(
        regular_kernel,
        grid_spec=pltpu.PrefetchScalarGridSpec(
            num_scalar_prefetch=1,
            grid=(heads,),
            in_specs=[smem, rows_in, rows_in, rows_in, rows_in, win_spec, glob_spec]
            + [random_spec(r) for r in range(ROUNDS)],
            out_specs=(rows_out, rows_out, own_spec, win_spec, win_spec, bits_spec, sink_spec),
            scratch_shapes=[pltpu.VMEM((bit_count, 2, tokens, HD), F32)],
        ),
        out_shape=(
            shape((tokens, width)),
            shape((tokens, width)),
            shape((2, tokens, width), F32),
            shape((2, 2, BLOCK, width)),
            shape((2, 2, BLOCK, width)),
            shape((bit_count, 2, tokens, width)),
            shape((heads, 8, 128), F32),
        ),
        compiler_params=params,
        cost_estimate=pl.CostEstimate(
            flops=4 * 10**9, bytes_accessed=2 * 10**7, transcendentals=3 * 10**6
        ),
        name="regular_rows",
    )(
        info,
        sink_logits,
        queries,
        key_rows,
        value_rows,
        out_grad,
        win,
        glob,
        bits,
        bits,
        bits,
    )

    own, red, sink_part = pl.pallas_call(
        global_kernel,
        grid_spec=pltpu.PrefetchScalarGridSpec(
            num_scalar_prefetch=1,
            grid=(heads,),
            in_specs=[
                smem,
                pl.BlockSpec((3, heads, 2 * BLOCK), lambda h, *_: (0, 0, 0)),
                glob_spec,
                rows_in,
                rows_in,
                own_spec,
                win_spec,
                sink_spec,
            ],
            out_specs=(own_spec, glob_spec, sink_spec),
        ),
        out_shape=(
            shape((2, tokens, width), F32),
            shape((2, 4, BLOCK, width)),
            shape((heads, 8, 128), F32),
        ),
        compiler_params=params,
        name="global_rows",
    )(info, sink_logits, all_stats, glob, key_rows, value_rows, own, dglob, sink_part)

    def give_back(kind, *args):
        return pl.pallas_call(
            functools.partial(return_kernel, n, bit_count, doc_bits, kind),
            out_shape=(
                shape((4, BLOCK, width)),
                shape((2, 2, BLOCK, width)),
                shape((bit_count, 2, tokens, width)),
                shape((heads, 8, 128), F32),
            ),
            in_specs=[vmem, any_spec, any_spec, vmem],
            out_specs=(vmem, any_spec, any_spec, vmem),
            scratch_shapes=[
                pltpu.VMEM((steps, heads, 8, 128), F32),
                pltpu.VMEM((steps, heads, 8, 128), F32),
                pltpu.VMEM((4, BLOCK, width), BF16),
                pltpu.VMEM((4, BLOCK, width), BF16),
                dma((4,)),
                dma((4,)),
                dma((4,)),
                dma((4,)),
            ]
            + side_sems
            + [dma((steps,)), dma((steps,))],
            compiler_params=pltpu.CompilerParams(
                collective_id=3 + kind, has_side_effects=True, vmem_limit_bytes=40 * 1024 * 1024
            ),
            name=f"return_blocks_{kind}",
        )(*args)

    red, rwin, rbits, sink_sum = lax.switch(
        mode, [functools.partial(give_back, kind) for kind in range(3)], red, dwin, dbits, sink_part
    )
    sink_grad = sink_sum[:, 0, 0] / math.sqrt(lax.axis_size("dp") * n * tokens)

    final_spec = pl.BlockSpec((1, tokens, HD), lambda h, *_: (0, 0, h))
    outs = pl.pallas_call(
        functools.partial(final_kernel, bit_count),
        grid_spec=pltpu.PrefetchScalarGridSpec(
            num_scalar_prefetch=1,
            grid=(heads,),
            in_specs=[
                rows_out,
                rows_out,
                own_spec,
                pl.BlockSpec((4, BLOCK, HD), lambda h, *_: (0, 0, h)),
                win_spec,
                bits_spec,
            ],
            out_specs=(final_spec,) * 4,
        ),
        out_shape=(shape((1, tokens, width)),) * 4,
        compiler_params=params,
        name="add_up",
    )(info, att, dq, own, red, rwin, rbits)
    return (*outs, sink_grad)


def solution(mesh):
    rows = P("dp", "ctx", "head")
    return jax.shard_map(
        body,
        mesh=mesh,
        in_specs=(rows, rows, rows, P("head"), P(), P("dp", None, None), rows),
        out_specs=(rows, rows, rows, rows, P("head")),
        check_vma=False,
    )
```

```python
import functools
import math

import jax
import jax.numpy as jnp
from jax import lax
from jax.experimental import pallas as pl
from jax.experimental.pallas import tpu as pltpu
from jax.sharding import PartitionSpec as P

HD = 128
BLOCK = 128
ROUNDS = 3
VARIED = 2
SCALE = HD ** (-0.5)
MESH = pl.DeviceIdType.MESH
F32 = jnp.float32
BF16 = jnp.bfloat16


def mm(a, b, ca, cb):
    return lax.dot_general(a, b, (((ca,), (cb,)), ((), ())), preferred_element_type=F32)


def flipped(place, bit):
    mask = 2**bit
    return place + mask * (1 - 2 * ((place // mask) % 2))


def greet(n, bit_count, me, doc_bits=0):
    barrier = pltpu.get_barrier_semaphore()
    for bit in range(bit_count):
        other = flipped(me, bit)
        pl.semaphore_signal(barrier, inc=1, device_id={"ctx": other}, device_id_type=MESH)
    for bit in range(doc_bits):
        other = flipped(lax.axis_index("dp"), bit)
        pl.semaphore_signal(barrier, inc=1, device_id={"dp": other}, device_id_type=MESH)
    for off in (-2, -1, 1, 2):
        other = me + off

        @pl.when((other >= 0) & (other < n))
        def _():
            pl.semaphore_signal(barrier, inc=1, device_id={"ctx": other}, device_id_type=MESH)

    inside = [((me + off >= 0) & (me + off < n)).astype(jnp.int32) for off in (-2, -1, 1, 2)]
    pl.semaphore_wait(barrier, bit_count + doc_bits + sum(inside))


def remote(src, dst, send, recv, target, axis="ctx"):
    return pltpu.make_async_remote_copy(
        src_ref=src,
        dst_ref=dst,
        send_sem=send,
        recv_sem=recv,
        device_id={axis: target},
        device_id_type=MESH,
    )


def exchange_sides(n, bits_used, me, lo_src, hi_src, lo_dst, hi_dst, bit_src, bit_dst, sems):
    ws, wr, bs, br = sems

    def lower(kv):
        return remote(lo_src(kv), hi_dst(kv), ws.at[0, kv], wr.at[1, kv], me - 1)

    def upper(kv):
        return remote(hi_src(kv), lo_dst(kv), ws.at[1, kv], wr.at[0, kv], me + 1)

    def bit_copy(bit, kv):
        other = flipped(me, bit)
        return remote(bit_src(bit, kv), bit_dst(bit, kv), bs.at[bit, kv], br.at[bit, kv], other)

    def start(up):
        for kv in range(2):
            if up:

                @pl.when(me < n - 1)
                def _():
                    upper(kv).start()

            else:

                @pl.when(me > 0)
                def _():
                    lower(kv).start()

        for bit in reversed(bits_used):
            if bit > 0:

                @pl.when((me // 2**bit) % 2 == (0 if up else 1))
                def _():
                    for kv in range(2):
                        bit_copy(bit, kv).start()

    def start_mate():
        for kv in range(2):
            bit_copy(0, kv).start()

    def wait():
        for kv in range(2):

            @pl.when(me > 0)
            def _():
                lower(kv).wait_send()
                upper(kv).wait_recv()

            @pl.when(me < n - 1)
            def _():
                upper(kv).wait_send()
                lower(kv).wait_recv()

        for bit in bits_used:
            for kv in range(2):
                bit_copy(bit, kv).wait()

    return start, start_mate, wait


def used_bits(bit_count, mode):
    return [bit for bit in range(bit_count) if bit != VARIED or mode > 0]


def part_of(ref, bit, kv, mode):
    if mode == 1 and bit == VARIED:
        return ref.at[bit, kv, pl.ds(0, BLOCK)]
    return ref.at[bit, kv]


def gather_kernel(n, bit_count, mode, *refs):
    q, k, v, g = refs[:4]
    packed = refs[4] if mode == 1 else None
    glob, win, bits, stats = refs[-16:-12]
    own_stats, got_stats, mate_s, next_s, glob_r, ws, wr, bs, br, local_s = refs[-12:-2]
    stat_s, stat_r = refs[-2:]
    me = lax.axis_index("ctx")
    side = me % 2
    tokens = q.shape[1]
    mate = me + 1 - 2 * side
    nxt = me + 2 - 4 * side
    source = side * (n - 1)
    has_next = (nxt >= 0) & (nxt < n)
    pair = (k, v)
    greet(n, bit_count, me)

    start, start_mate, wait = exchange_sides(
        n,
        used_bits(bit_count, mode),
        me,
        lambda kv: pair[kv].at[0, pl.ds(0, BLOCK)],
        lambda kv: pair[kv].at[0, pl.ds(tokens - BLOCK, BLOCK)],
        lambda kv: win.at[0, kv],
        lambda kv: win.at[1, kv],
        lambda bit, kv: packed.at[kv] if mode == 1 and bit == VARIED else pair[kv].at[0],
        lambda bit, kv: part_of(bits, bit, kv, mode),
        (ws, wr, bs, br),
    )
    first_row = side * (tokens - BLOCK)

    def own_copy(j):
        ref = (q, k, v, g)[j]
        return pltpu.make_async_copy(
            ref.at[0, pl.ds(pl.multiple_of(first_row, BLOCK), BLOCK)], glob.at[side, j], local_s.at[j]
        )

    def to_mate(j, s):
        return remote(glob.at[s, j], glob.at[s, j], mate_s.at[j], glob_r.at[s, j], mate)

    def to_next(j):
        return remote(glob.at[side, j], glob.at[side, j], next_s.at[j], glob_r.at[side, j], nxt)

    order = (0, 3, 1, 2)
    is_source = me == source

    def phase(chain):
        @pl.when((side == chain) & is_source)
        def _():
            for j in order:
                own_copy(j).start()
            for j in order:
                own_copy(j).wait()
                to_next(j).start()
                to_mate(j, side).start()

        @pl.when((side == chain) & jnp.logical_not(is_source))
        def _():
            for j in order:
                to_next(j).wait_recv()

                @pl.when(has_next)
                def _():
                    to_next(j).start()

                to_mate(j, side).start()

        @pl.when(side != chain)
        def _():
            for j in order:
                to_mate(j, 1 - side).wait_recv()

        start(chain == 0)

    start_mate()

    @pl.when(me < n // 2)
    def _():
        phase(0)
        phase(1)

    @pl.when(me >= n // 2)
    def _():
        phase(1)
        phase(0)

    for j in order:
        to_mate(j, side).wait_send()

        @pl.when(has_next)
        def _():
            to_next(j).wait_send()

    for h in range(q.shape[2] // HD):
        cols = slice(h * HD, (h + 1) * HD)
        gq = jnp.concatenate([glob[0, 0, :, cols], glob[1, 0, :, cols]], axis=0)
        gg = jnp.concatenate([glob[0, 3, :, cols], glob[1, 3, :, cols]], axis=0)
        s = mm(k[0, :, cols], gq, 1, 1) * SCALE
        top = jnp.max(s, axis=0, keepdims=True)
        expo = jnp.exp(s - top)
        dp = mm(v[0, :, cols], gg, 1, 1)
        own_stats[0, 0, h : h + 1, :] = top
        own_stats[0, 1, h : h + 1, :] = jnp.sum(expo, axis=0, keepdims=True)
        own_stats[0, 2, h : h + 1, :] = jnp.sum(
            expo.astype(BF16).astype(F32) * dp, axis=0, keepdims=True
        )

    def swap(bit):
        return remote(
            own_stats.at[bit], got_stats.at[bit], stat_s.at[bit], stat_r.at[bit], flipped(me, bit)
        )

    for bit in range(bit_count):
        swap(bit).start()
        swap(bit).wait_recv()
        top = jnp.maximum(own_stats[bit, 0], got_stats[bit, 0])
        mine = jnp.exp(own_stats[bit, 0] - top)
        other = jnp.exp(got_stats[bit, 0] - top)
        merged = [top] + [own_stats[bit, i] * mine + got_stats[bit, i] * other for i in (1, 2)]
        for i in range(3):
            if bit < bit_count - 1:
                own_stats[bit + 1, i] = merged[i]
            else:
                stats[i] = merged[i]
    for bit in range(bit_count):
        swap(bit).wait_send()
    wait()


def return_kernel(
    n,
    bit_count,
    doc_bits,
    mode,
    red,
    dwin,
    dbits,
    sink_in,
    red_out,
    rwin,
    rbits,
    sink_out,
    sink_send,
    sink_recv,
    mate_buf,
    chain_buf,
    mate_s,
    mate_r,
    next_s,
    chain_r,
    ws,
    wr,
    bs,
    br,
    sink_s,
    sink_r,
    passed,
):
    me = lax.axis_index("ctx")
    side = me % 2
    mate = me + 1 - 2 * side
    nxt = me - 2 + 4 * side
    prv = me + 2 - 4 * side
    has_next = (nxt >= 0) & (nxt < n)
    has_prev = (prv >= 0) & (prv < n)
    greet(n, bit_count, me, doc_bits)

    start, start_mate, wait = exchange_sides(
        n,
        used_bits(bit_count, mode),
        me,
        lambda kv: dwin.at[0, kv],
        lambda kv: dwin.at[1, kv],
        lambda kv: rwin.at[0, kv],
        lambda kv: rwin.at[1, kv],
        lambda bit, kv: part_of(dbits, bit, kv, mode),
        lambda bit, kv: part_of(rbits, bit, kv, mode),
        (ws, wr, bs, br),
    )

    def to_mate(j):
        return remote(red.at[1 - side, j], mate_buf.at[j], mate_s.at[j], mate_r.at[j], mate)

    def to_next(j):
        return remote(red_out.at[j], chain_buf.at[j], next_s.at[j], chain_r.at[j], nxt)

    for j in range(4):
        to_mate(j).start()
    start_mate()

    def phase(chain):
        @pl.when(side == chain)
        def _():
            for j in range(4):
                to_mate(j).wait_recv()

                @pl.when(jnp.logical_not(has_prev))
                def _():
                    total = red[side, j].astype(F32) + mate_buf[j].astype(F32)
                    red_out[j] = total.astype(BF16)

                @pl.when(has_prev)
                def _():
                    to_next(j).wait_recv()
                    total = red[side, j].astype(F32) + mate_buf[j].astype(F32)
                    red_out[j] = (total + chain_buf[j].astype(F32)).astype(BF16)

                @pl.when(has_next)
                def _():
                    to_next(j).start()

            pl.semaphore_signal(passed, inc=1, device_id={"ctx": mate}, device_id_type=MESH)

        @pl.when(side != chain)
        def _():
            pl.semaphore_wait(passed, 1)

        start(chain == 1)

    @pl.when(me < n // 2)
    def _():
        phase(1)
        phase(0)

    @pl.when(me >= n // 2)
    def _():
        phase(0)
        phase(1)

    for j in range(4):
        to_mate(j).wait_send()

        @pl.when(has_next)
        def _():
            to_next(j).wait_send()

    steps = bit_count + doc_bits

    def swap(i):
        if i < doc_bits:
            axis, target = "dp", flipped(lax.axis_index("dp"), i)
        else:
            axis, target = "ctx", flipped(me, i - doc_bits)
        return remote(sink_send.at[i], sink_recv.at[i], sink_s.at[i], sink_r.at[i], target, axis)

    sink_send[0] = sink_in[...]
    for i in range(steps):
        swap(i).start()
        swap(i).wait_recv()
        total = sink_send[i] + sink_recv[i]
        if i < steps - 1:
            sink_send[i + 1] = total
        else:
            sink_out[...] = total
    for i in range(steps):
        swap(i).wait_send()
    wait()


def regular_kernel(
    info,
    sink_ref,
    q,
    k,
    v,
    g,
    win,
    glob,
    r0,
    r1,
    r2,
    att,
    dq,
    own,
    dwin,
    dglob,
    dbits,
    sink_out,
    racc,
):
    head = pl.program_id(0)
    is_first = info[6] == 1
    is_last = info[7] == 1
    sink = sink_ref[head]
    tokens = q.shape[1]
    count = tokens // BLOCK
    randoms = (r0, r1, r2)
    ext, shared = [], []
    for kv, ref in enumerate((k, v)):
        lo = jnp.where(is_first, jnp.zeros((BLOCK, HD), BF16), win[0, kv])
        hi = jnp.where(is_last, jnp.zeros((BLOCK, HD), BF16), win[1, kv])
        ext.append([lo] + [ref[0, i * BLOCK : (i + 1) * BLOCK] for i in range(count)] + [hi])
        shared.append([glob[0, 1 + kv], glob[1, 1 + kv]] + [r[0, kv] for r in randoms])
    slots = 5 + ROUNDS
    col = lax.broadcasted_iota(jnp.int32, (BLOCK, slots * BLOCK), 1)
    ext_grad = [[None] * (count + 2), [None] * (count + 2)]
    shared_grad = [None, None]
    sink_sum = jnp.zeros((1, 1), F32)
    for b in range(count):
        keys = jnp.concatenate(ext[0][b : b + 3] + shared[0], axis=0)
        vals = jnp.concatenate(ext[1][b : b + 3] + shared[1], axis=0)
        rows = slice(b * BLOCK, (b + 1) * BLOCK)
        qb, gb = q[0, rows], g[0, rows]
        s = mm(qb, keys, 1, 1) * SCALE
        if b == 1:
            s = jnp.where(is_first & (col < BLOCK), -jnp.inf, s)
        if b == count - 2:
            s = jnp.where(is_last & (col >= 2 * BLOCK) & (col < 3 * BLOCK), -jnp.inf, s)
        top = jnp.maximum(jnp.max(s, axis=1, keepdims=True), sink)
        expo = jnp.exp(s - top)
        at_sink = jnp.exp(sink - top)
        total = at_sink + jnp.sum(expo, axis=1, keepdims=True)
        inv = 1.0 / total
        out = (mm(expo.astype(BF16), vals, 1, 0) * inv).astype(BF16)
        att[rows, :] = out
        delta = jnp.sum(gb.astype(F32) * out.astype(F32), axis=1, keepdims=True)
        keep = None
        if b == 0:
            keep = jnp.logical_not(is_first)
        if b == count - 1:
            last_ok = jnp.logical_not(is_last)
            keep = last_ok if keep is None else keep & last_ok
        if keep is not None:
            inv = jnp.where(keep, inv, 0.0)
        probs = expo * inv
        dp = mm(gb, vals, 1, 1)
        ds = (probs * (dp - delta)).astype(BF16)
        ph = probs.astype(BF16)
        sink_sum = sink_sum - jnp.sum(at_sink * inv * delta, axis=0, keepdims=True)
        dq[rows, :] = (mm(ds, keys, 1, 0) * SCALE).astype(BF16)
        for kv, full in enumerate((mm(ds, qb, 0, 0) * SCALE, mm(ph, gb, 0, 0))):
            for i in range(3):
                part = full[i * BLOCK : (i + 1) * BLOCK]
                old = ext_grad[kv][b + i]
                ext_grad[kv][b + i] = part if old is None else old + part
            rest = full[3 * BLOCK :]
            shared_grad[kv] = rest if shared_grad[kv] is None else shared_grad[kv] + rest
    racc[...] = jnp.zeros_like(racc)
    for kv in range(2):
        dwin[0, kv] = ext_grad[kv][0].astype(BF16)
        dwin[1, kv] = ext_grad[kv][count + 1].astype(BF16)
        for i in range(count):
            own[kv, i * BLOCK : (i + 1) * BLOCK, :] = ext_grad[kv][i + 1]
        dglob[0, kv] = shared_grad[kv][:BLOCK].astype(BF16)
        dglob[1, kv] = shared_grad[kv][BLOCK : 2 * BLOCK].astype(BF16)
        for r in range(ROUNDS):
            at = pl.ds(pl.multiple_of(info[ROUNDS + r] * BLOCK, BLOCK), BLOCK)
            racc[info[r], kv, at, :] += shared_grad[kv][(2 + r) * BLOCK : (3 + r) * BLOCK]
    dbits[...] = racc[...].astype(BF16)
    sink_out[0] = jnp.broadcast_to(sink_sum, (8, 128))


def global_kernel(info, sink_ref, stats, glob, k, v, own, dglob, sink_in, own_out, red, sink_out):
    head = pl.program_id(0)
    sink = sink_ref[head]
    is_first = info[6] == 1
    is_last = info[7] == 1
    gq = jnp.concatenate([glob[0, 0], glob[1, 0]], axis=0)
    gg = jnp.concatenate([glob[0, 3], glob[1, 3]], axis=0)
    row = pl.ds(head, 1)
    shard_top = stats[0, row, :]
    top = jnp.maximum(shard_top, sink)
    at_sink = jnp.exp(sink - top)
    ratio = jnp.exp(shard_top - top)
    inv = 1.0 / (at_sink + stats[1, row, :] * ratio)
    delta = stats[2, row, :] * ratio * inv
    s = mm(k[0], gq, 1, 1) * SCALE
    probs = jnp.exp(s - top) * inv
    dp = mm(v[0], gg, 1, 1)
    ds = (probs * (dp - delta)).astype(BF16)
    ph = probs.astype(BF16)
    own_out[0] = own[0] + mm(ds, gq, 1, 0) * SCALE
    own_out[1] = own[1] + mm(ph, gg, 1, 0)
    out = mm(ph, v[0], 0, 0).astype(BF16)
    gdq = (mm(ds, k[0], 0, 0) * SCALE).astype(BF16)
    for s_ in range(2):
        rows = slice(s_ * BLOCK, (s_ + 1) * BLOCK)
        red[s_, 0] = out[rows]
        red[s_, 1] = gdq[rows]
        red[s_, 2] = dglob[s_, 0]
        red[s_, 3] = dglob[s_, 1]
    terms = at_sink * inv * delta
    lane = lax.broadcasted_iota(jnp.int32, terms.shape, 1)
    mine = (is_first & (lane < BLOCK)) | (is_last & (lane >= BLOCK))
    part = jnp.sum(jnp.where(mine, terms, 0.0), axis=1, keepdims=True)
    sink_out[0] = sink_in[0] - jnp.broadcast_to(part, (8, 128))


def final_kernel(bit_count, info, att, dq, own, red, rwin, rbits, att_o, dq_o, dk_o, dv_o):
    is_first = info[6] == 1
    is_last = info[7] == 1
    tokens = att.shape[0]
    count = tokens // BLOCK
    for b in range(count):
        rows = slice(b * BLOCK, (b + 1) * BLOCK)
        a, d = att[rows, :], dq[rows, :]
        grads = [own[kv, rows, :] for kv in range(2)]
        for bit in range(bit_count):
            for kv in range(2):
                term = rbits[bit, kv, rows, :]
                if bit == VARIED:
                    single = (info[8] == 1) & (info[9] == b)
                    term = jnp.where(info[8] == 2, term, jnp.zeros_like(term))
                    term = jnp.where(single, rbits[bit, kv, :BLOCK, :], term)
                grads[kv] = grads[kv] + term.astype(F32)
        for edge, here, side in ((0, is_first, 0), (count - 1, is_last, 1)):
            if b == edge:
                a = jnp.where(here, red[0], a)
                d = jnp.where(here, red[1], d)
                for kv in range(2):
                    grads[kv] = grads[kv] + jnp.where(here, red[2 + kv], rwin[side, kv]).astype(F32)
        att_o[0, rows, :] = a
        dq_o[0, rows, :] = d
        dk_o[0, rows, :] = grads[0].astype(BF16)
        dv_o[0, rows, :] = grads[1].astype(BF16)


def body(queries, key_rows, value_rows, sink_logits, partner, block_pick, out_grad):
    _, tokens, width = queries.shape
    heads = width // HD
    n = lax.axis_size("ctx")
    bit_count = n.bit_length() - 1
    me = lax.axis_index("ctx")
    any_spec = pl.BlockSpec(memory_space=pl.ANY)
    dma = pltpu.SemaphoreType.DMA
    masks = partner[:, 0]
    bit_of = sum(b * (jnp.right_shift(masks, b) & 1) for b in range(bit_count))
    place = jnp.bitwise_xor(me, masks)
    ids = jnp.arange(n)[None, :]
    picked = jnp.sum(jnp.where(ids == me, block_pick[0], 0), axis=1)
    asked = jnp.sum(jnp.where(ids == place[:, None], block_pick[0], 0), axis=1)
    varied = bit_of == VARIED
    mode = jnp.minimum(jnp.sum(varied.astype(jnp.int32)), 2)
    slot = jnp.where(varied & (mode == 1), 0, picked)
    asked_block = jnp.where(mode == 1, jnp.sum(jnp.where(varied, asked, 0)), 0)
    extra = jnp.stack([(me == 0) * 1, (me == n - 1) * 1, mode, asked_block])
    info = jnp.concatenate([bit_of, slot, extra]).astype(jnp.int32)
    doc_bits = lax.axis_size("dp").bit_length() - 1
    steps = bit_count + doc_bits
    params = pltpu.CompilerParams(vmem_limit_bytes=40 * 1024 * 1024)
    vmem = pl.BlockSpec(memory_space=pltpu.VMEM)
    side_sems = [dma((2, 2)), dma((2, 2)), dma((bit_count, 2)), dma((bit_count, 2))]

    def shape(dims, dtype=BF16):
        return jax.ShapeDtypeStruct(dims, dtype)

    def gather(kind, q, k, v, g):
        args = [q, k, v, g]
        if kind == 1:
            start = (0, asked_block * BLOCK, 0)
            cut = [lax.dynamic_slice(rows, start, (1, BLOCK, width)) for rows in (k, v)]
            args.append(jnp.concatenate(cut, axis=0))
        return pl.pallas_call(
            functools.partial(gather_kernel, n, bit_count, kind),
            out_shape=(
                shape((2, 4, BLOCK, width)),
                shape((2, 2, BLOCK, width)),
                shape((bit_count, 2, tokens, width)),
                shape((3, heads, 2 * BLOCK), F32),
            ),
            in_specs=[any_spec, vmem, vmem, any_spec] + [any_spec] * (len(args) - 4),
            out_specs=(vmem, any_spec, any_spec, vmem),
            scratch_shapes=[
                pltpu.VMEM((bit_count, 3, heads, 2 * BLOCK), F32),
                pltpu.VMEM((bit_count, 3, heads, 2 * BLOCK), F32),
                dma((4,)),
                dma((4,)),
                dma((2, 4)),
            ]
            + side_sems
            + [dma((4,)), dma((bit_count,)), dma((bit_count,))],
            compiler_params=pltpu.CompilerParams(
                collective_id=kind, has_side_effects=True, vmem_limit_bytes=40 * 1024 * 1024
            ),
            name=f"gather_blocks_{kind}",
        )(*args)

    glob, win, bits, all_stats = lax.switch(
        mode,
        [functools.partial(gather, kind) for kind in range(3)],
        queries,
        key_rows,
        value_rows,
        out_grad,
    )

    smem = pl.BlockSpec(memory_space=pltpu.SMEM)
    rows_in = pl.BlockSpec((1, tokens, HD), lambda h, *_: (0, 0, h))
    rows_out = pl.BlockSpec((tokens, HD), lambda h, *_: (0, h))
    own_spec = pl.BlockSpec((2, tokens, HD), lambda h, *_: (0, 0, h))
    glob_spec = pl.BlockSpec((2, 4, BLOCK, HD), lambda h, *_: (0, 0, 0, h))
    win_spec = pl.BlockSpec((2, 2, BLOCK, HD), lambda h, *_: (0, 0, 0, h))
    bits_spec = pl.BlockSpec((bit_count, 2, tokens, HD), lambda h, *_: (0, 0, 0, h))
    sink_spec = pl.BlockSpec((1, 8, 128), lambda h, *_: (h, 0, 0))
    def random_spec(r):
        return pl.BlockSpec(
            (1, 2, BLOCK, HD), lambda h, info: (info[r], 0, info[ROUNDS + r], h)
        )

    att, dq, own, dwin, dglob, dbits, sink_part = pl.pallas_call(
        regular_kernel,
        grid_spec=pltpu.PrefetchScalarGridSpec(
            num_scalar_prefetch=1,
            grid=(heads,),
            in_specs=[smem, rows_in, rows_in, rows_in, rows_in, win_spec, glob_spec]
            + [random_spec(r) for r in range(ROUNDS)],
            out_specs=(rows_out, rows_out, own_spec, win_spec, win_spec, bits_spec, sink_spec),
            scratch_shapes=[pltpu.VMEM((bit_count, 2, tokens, HD), F32)],
        ),
        out_shape=(
            shape((tokens, width)),
            shape((tokens, width)),
            shape((2, tokens, width), F32),
            shape((2, 2, BLOCK, width)),
            shape((2, 2, BLOCK, width)),
            shape((bit_count, 2, tokens, width)),
            shape((heads, 8, 128), F32),
        ),
        compiler_params=params,
        cost_estimate=pl.CostEstimate(
            flops=4 * 10**9, bytes_accessed=2 * 10**7, transcendentals=3 * 10**6
        ),
        name="regular_rows",
    )(
        info,
        sink_logits,
        queries,
        key_rows,
        value_rows,
        out_grad,
        win,
        glob,
        bits,
        bits,
        bits,
    )

    own, red, sink_part = pl.pallas_call(
        global_kernel,
        grid_spec=pltpu.PrefetchScalarGridSpec(
            num_scalar_prefetch=1,
            grid=(heads,),
            in_specs=[
                smem,
                pl.BlockSpec((3, heads, 2 * BLOCK), lambda h, *_: (0, 0, 0)),
                glob_spec,
                rows_in,
                rows_in,
                own_spec,
                win_spec,
                sink_spec,
            ],
            out_specs=(own_spec, glob_spec, sink_spec),
        ),
        out_shape=(
            shape((2, tokens, width), F32),
            shape((2, 4, BLOCK, width)),
            shape((heads, 8, 128), F32),
        ),
        compiler_params=params,
        name="global_rows",
    )(info, sink_logits, all_stats, glob, key_rows, value_rows, own, dglob, sink_part)

    def give_back(kind, *args):
        return pl.pallas_call(
            functools.partial(return_kernel, n, bit_count, doc_bits, kind),
            out_shape=(
                shape((4, BLOCK, width)),
                shape((2, 2, BLOCK, width)),
                shape((bit_count, 2, tokens, width)),
                shape((heads, 8, 128), F32),
            ),
            in_specs=[vmem, any_spec, any_spec, vmem],
            out_specs=(vmem, any_spec, any_spec, vmem),
            scratch_shapes=[
                pltpu.VMEM((steps, heads, 8, 128), F32),
                pltpu.VMEM((steps, heads, 8, 128), F32),
                pltpu.VMEM((4, BLOCK, width), BF16),
                pltpu.VMEM((4, BLOCK, width), BF16),
                dma((4,)),
                dma((4,)),
                dma((4,)),
                dma((4,)),
            ]
            + side_sems
            + [dma((steps,)), dma((steps,)), pltpu.SemaphoreType.REGULAR],
            compiler_params=pltpu.CompilerParams(
                collective_id=3 + kind, has_side_effects=True, vmem_limit_bytes=40 * 1024 * 1024
            ),
            name=f"return_blocks_{kind}",
        )(*args)

    red, rwin, rbits, sink_sum = lax.switch(
        mode, [functools.partial(give_back, kind) for kind in range(3)], red, dwin, dbits, sink_part
    )
    sink_grad = sink_sum[:, 0, 0] / math.sqrt(lax.axis_size("dp") * n * tokens)

    final_spec = pl.BlockSpec((1, tokens, HD), lambda h, *_: (0, 0, h))
    outs = pl.pallas_call(
        functools.partial(final_kernel, bit_count),
        grid_spec=pltpu.PrefetchScalarGridSpec(
            num_scalar_prefetch=1,
            grid=(heads,),
            in_specs=[
                rows_out,
                rows_out,
                own_spec,
                pl.BlockSpec((4, BLOCK, HD), lambda h, *_: (0, 0, h)),
                win_spec,
                bits_spec,
            ],
            out_specs=(final_spec,) * 4,
        ),
        out_shape=(shape((1, tokens, width)),) * 4,
        compiler_params=params,
        name="add_up",
    )(info, att, dq, own, red, rwin, rbits)
    return (*outs, sink_grad)


def solution(mesh):
    rows = P("dp", "ctx", "head")
    return jax.shard_map(
        body,
        mesh=mesh,
        in_specs=(rows, rows, rows, P("head"), P(), P("dp", None, None), rows),
        out_specs=(rows, rows, rows, rows, P("head")),
        check_vma=False,
    )
```
